256 devices in a mesh: dp: 64 (over z, x, core), tensor: 4 (over y).
Axes of the slice: x: 4, y: 4, z: 8, core: 2. Of those that a mesh axis runs over, the one named last changes fastest.
Arguments:
- acts: bfloat16 [32768, 8192], P(('dp', 'tensor')), may hold values from -6 to 6
- key_grad: bfloat16 [32768, 512], P('dp', 'tensor'), may hold values from -0.625 to 0.625
- key_weight: bfloat16 [8192, 512], P(None, 'tensor'), may hold values from -0.5 to 0.5
- feedback: bfloat16 [64, 8192, 512], P('dp', None, 'tensor'), may hold values from -6 to 6
- factor_start: float32 [512, 64], P('tensor'), may hold values from -6 to 6
Outputs:
- rebuilt_grad: bfloat16 [8192, 512], P(None, 'tensor')
- feedback_next: bfloat16 [64, 8192, 512], P('dp', None, 'tensor')
- factor_next: float32 [512, 64], P('tensor')
- input_grad: bfloat16 [32768, 8192], P(('dp', 'tensor'))
The draws below stay inside these ranges and needn't reach their ends.
All inputs are finite; a program needn't handle non-finite values.
Results may differ from the reference program's by a relative error of at most 0.013.
Values may be sent and summed in bfloat16 or wider, within the bound.
No kernel may reach another device: no remote copies, remote signals or barrier semaphores. Data moves between devices by JAX's collectives and lax.ppermute only.
A program may use at most 128 MiB of HBM per device.

```python
import jax
import jax.numpy as jnp
from jax import lax

D = 8192
HD = 128
KV_HEADS = 4
KV_WIDTH = 512
RANK = 64
TOK_DEV = 512
TOKENS = 32768
N_DP = 64


def shard_levels(key, shape, cuts, smallest, largest):
    level, own = 1.0, jax.random.fold_in(key, 6)
    for position, blocks in cuts:
        steps = jnp.exp(jax.random.uniform(jax.random.fold_in(own, position), (blocks,), jnp.float32, smallest / len(cuts), largest / len(cuts)))
        level = level * jnp.repeat(steps, shape[position] // blocks).reshape([-1 if axis == position else 1 for axis in range(len(shape))])
    return level


def gaussian(key, dims, width, bound, pieces=(), kind=jnp.bfloat16):
    entries = width * jax.random.normal(key, dims, jnp.float32)
    if pieces:
        entries = entries * shard_levels(key, dims, pieces, -0.22, 0.18)
    return jnp.clip(entries, -bound, bound).astype(kind)


def setup_inputs(seed: int = 0) -> dict:
    streams_of = jax.random.split(jax.random.key(seed), 6)
    return {
        "acts": gaussian(streams_of[0], (TOKENS, D), 1.0, 6.0, ((0, 256),)),
        "key_grad": gaussian(streams_of[1], (TOKENS, KV_WIDTH), 0.1, 0.625, ((0, 64), (1, 4))),
        "key_weight": gaussian(streams_of[2], (D, KV_WIDTH), HD ** -0.5, 0.5, ((1, 4),)),
        "feedback": gaussian(streams_of[3], (N_DP, D, KV_WIDTH), 1.0, 6.0, ((0, 64), (2, 4))),
        "factor_start": gaussian(streams_of[4], (KV_WIDTH, RANK), 1.0, 6.0, ((0, 4),), jnp.float32),
    }


def solve_head(triangle, columns):
    return lax.linalg.triangular_solve(triangle, columns, left_side=False, lower=True, transpose_a=True)

def reference(acts, key_grad, key_weight, feedback, factor_start):
    highest = lax.Precision.HIGHEST
    act_blocks = acts.reshape(N_DP, TOK_DEV, D)
    grad_blocks = key_grad.reshape(N_DP, TOK_DEV, KV_HEADS * HD)

    def merge_replica(triple):
        row_block, grad_rows, saved = triple
        return jnp.dot(row_block.T.astype(jnp.float32), grad_rows.astype(jnp.float32), preferred_element_type=jnp.float32) + saved.astype(jnp.float32)
    merged = lax.map(merge_replica, (act_blocks, grad_blocks, feedback))
    by_head = merged.reshape(N_DP, D, KV_HEADS, HD)
    warm_start = factor_start.reshape(KV_HEADS, HD, RANK)
    projected = jnp.einsum('wdkh,khr->dkr', by_head, warm_start, precision=highest)
    gram_matrix = jnp.einsum('dkr,dks->krs', projected, projected, precision=highest)
    triangle = jnp.linalg.cholesky(gram_matrix)
    orthonormal = jax.vmap(solve_head, in_axes=(0, 1), out_axes=1)(triangle, projected)
    summed = jnp.einsum('wdkh,dkr->khr', by_head, orthonormal, precision=highest)
    mean_factor = summed / N_DP
    rebuilt = jnp.einsum('dkr,khr->dkh', orthonormal, mean_factor, precision=highest).reshape(D, KV_HEADS * HD)
    new_feedback = (merged - rebuilt[None]).astype(jnp.bfloat16)
    weights = key_weight.reshape(D, KV_HEADS, HD).astype(jnp.float32)

    def input_replica(grad_rows):
        head_rows = grad_rows.reshape(TOK_DEV, KV_HEADS, HD).astype(jnp.float32)
        partials = jnp.einsum('tkh,dkh->ktd', head_rows, weights).astype(jnp.bfloat16)
        partials = lax.optimization_barrier(partials)
        return jnp.sum(partials.astype(jnp.float32), axis=0).astype(jnp.bfloat16)
    input_grad = lax.map(input_replica, grad_blocks).reshape(TOKENS, D)
    return (rebuilt.astype(jnp.bfloat16), new_feedback, mean_factor.reshape(KV_HEADS * HD, RANK), input_grad)
```

```python
import jax
import jax.numpy as jnp
from jax import lax
from jax.experimental import pallas as pl
from jax.experimental.pallas import tpu as pltpu
from jax.sharding import PartitionSpec as P

BF16 = jnp.bfloat16
F32 = jnp.float32
HIGHEST = lax.Precision.HIGHEST
NZ, NX, NC, NY = 8, 4, 2, 4
D, HD, RANK, TOK, REPLICAS = 8192, 128, 64, 128, 64
QUARTER = D // NY
STEP = D // 8


def move(value, dz=0, dx=0, dc=0):
    perm = []
    for z in range(NZ):
        for x in range(NX):
            for c in range(NC):
                target = (((z + dz) % NZ) * NX + (x + dx) % NX) * NC + (c + dc) % NC
                perm.append(((z * NX + x) * NC + c, target))
    return lax.ppermute(value, "dp", perm)


def move_y(value, dy):
    return lax.ppermute(value, "tensor", [(i, (i + dy) % NY) for i in range(NY)])


def take(blocks, index, axis=0):
    return lax.dynamic_index_in_dim(blocks, index, axis, keepdims=False)


def after(value, *others):
    return lax.optimization_barrier((value, *others))[0]


def tdot(left, right):
    return lax.dot_general(left, right, (((0,), (0,)), ((), ())), preferred_element_type=F32)


def reduce_blocks(parts, z, x, c):
    acc = take(parts, c, 1).astype(F32) + move(take(parts, 1 - c, 1).astype(BF16), dc=1).astype(F32)
    sent = [move(take(acc, (x + d) % NX, 1).astype(BF16), dx=d) for d in (2, 1, 3)]
    acc = take(acc, x, 1)
    for piece in sent:
        acc = acc + piece.astype(F32)
    rel = {o: take(acc, (z + o) % NZ, 1) for o in range(-4, 4)}
    up = move(jnp.stack([rel[2], rel[3], rel[-4]]).astype(BF16), dz=3).astype(F32)
    down = move(jnp.stack([rel[-2], rel[-3]]).astype(BF16), dz=-3).astype(F32)
    low = rel[-1] + up[0]
    own = rel[0] + up[1] + down[1]
    high = rel[1] + up[2] + down[0]
    from_below = move(high.astype(BF16), dz=1)
    from_above = move(low.astype(BF16), dz=-1)
    return own + from_below.astype(F32) + from_above.astype(F32)


def gather_blocks(block, z, x, c):
    below = move(block, dz=1)
    above = move(block, dz=-1)
    far_below = move(jnp.stack([below, block, above]), dz=3)
    far_above = move(jnp.stack([below, block]), dz=-3)
    ring = jnp.concatenate([far_below, jnp.stack([below, block, above]), far_above])
    column = jnp.roll(ring, z - 4, axis=0)
    others = [move(column, dx=d) for d in (2, 1, 3)]
    ring = jnp.stack([others[2], others[0], others[1], column])
    half = jnp.roll(ring, x - 3, axis=0)
    other = move(half, dc=1)
    return jnp.stack([jnp.where(c == 0, half, other), jnp.where(c == 0, other, half)])


def finish_kernel(sums_ref, start_ref, merged_ref, rebuilt_ref, feedback_ref, factor_ref, high_ref, low_ref, rows_ref):
    step = pl.program_id(0)

    @pl.when(step == 0)
    def _():
        gram_all = jnp.zeros((HD, HD), F32)
        for c in range(NC):
            for q in range(NY):
                rows = sums_ref[c, :, q].reshape(STEP, HD)
                gram_all = gram_all + tdot(rows, rows)
        start = start_ref[...]
        start_t = start.T
        projected = jnp.dot(start_t, gram_all, precision=HIGHEST, preferred_element_type=F32)
        gram = jnp.dot(projected, start, precision=HIGHEST, preferred_element_type=F32)
        table = jnp.concatenate([gram, gram, projected, start_t], axis=1)
        for k in range(RANK):
            base = k // 8 * 8
            table = table[-(RANK - base) :] if table.shape[0] > RANK - base else table
            local = k - base
            scale = 1.0 / jnp.sqrt(table[local : local + 1, k : k + 1])
            row = table[local : local + 1, :] * scale
            rows_ref[k : k + 1, :] = row[:, HD:]
            if k + 1 < RANK:
                column = table[:, k : k + 1] * scale
                below = lax.broadcasted_iota(jnp.int32, column.shape, 0) > local
                table = table - jnp.where(below, column, 0.0) * row
        right = rows_ref[:, :HD]
        left = rows_ref[:, HD:]
        kernel = lax.dot_general(
            left, right, (((0,), (0,)), ((), ())), precision=HIGHEST, preferred_element_type=F32
        ) * (1.0 / REPLICAS)
        factor_ref[...] = right.T * (1.0 / REPLICAS)
        high = kernel.astype(BF16)
        high_ref[...] = high
        low_ref[...] = (kernel - high.astype(F32)).astype(BF16)

    rows = sums_ref[step % NC, :, step // NC].reshape(STEP, HD)
    rebuilt = jnp.dot(rows, high_ref[...], preferred_element_type=F32)
    rebuilt = rebuilt + jnp.dot(rows, low_ref[...], preferred_element_type=F32)
    rebuilt_ref[...] = rebuilt.astype(BF16)
    feedback_ref[...] = (merged_ref[...] - rebuilt).astype(BF16)


def finish(sums, factor_start, merged):
    whole = lambda *shape: pl.BlockSpec(shape, lambda i: (0,) * len(shape))
    part = pl.BlockSpec((STEP, HD), lambda i: (i, 0))
    return pl.pallas_call(
        finish_kernel,
        grid=(D // STEP,),
        in_specs=[whole(NC, NX * NZ, NY, D // 256, HD), whole(HD, RANK), part],
        out_specs=[part, part, whole(HD, RANK)],
        out_shape=[
            jax.ShapeDtypeStruct((D, HD), BF16),
            jax.ShapeDtypeStruct((D, HD), BF16),
            jax.ShapeDtypeStruct((HD, RANK), F32),
        ],
        scratch_shapes=[
            pltpu.VMEM((HD, HD), BF16),
            pltpu.VMEM((HD, HD), BF16),
            pltpu.VMEM((RANK, 2 * HD), F32),
        ],
        compiler_params=pltpu.CompilerParams(vmem_limit_bytes=24 * 2**20),
        cost_estimate=pl.CostEstimate(flops=10**9, bytes_accessed=12 * 2**20, transcendentals=0),
    )(sums, factor_start, merged)


def shards(acts, key_grad, key_weight, feedback, factor_start):
    dp = lax.axis_index("dp")
    y = lax.axis_index("tensor")
    z, x, c = dp // (NX * NC), (dp // NC) % NX, dp % NC

    heads = [key_grad, None, None, None]
    for d in (1, 3, 2):
        heads[(NY - d) % NY] = move_y(key_grad, d)
    grad_rows = jnp.concatenate(heads, axis=1).reshape(NY, TOK, NY * HD)
    grad_rows = jnp.roll(grad_rows, -y, axis=0)

    columns = [acts[:, i * QUARTER : (i + 1) * QUARTER] for i in range(NY)]
    quarter = lambda i: lax.select_n(i % NY, *columns)
    tokens = [quarter(y), None, None, None]
    for d in (2, 1, 3):
        tokens[(NY - d) % NY] = move_y(quarter(y + d), d)
    partial = sum(tdot(tokens[j], grad_rows[j]) for j in range(NY))
    summed = reduce_blocks(partial.reshape(1, NC, NX, NZ, 32, NY * HD), z, x, c)[0]

    saved = reduce_blocks(feedback.reshape(NY, NC, NX, NZ, 32, HD), z, x, c)

    ring = [summed[:, :HD]] + [move_y(summed[:, j * HD : (j + 1) * HD], j) for j in (1, 2, 3)]
    block = jnp.roll(jnp.stack(ring[::-1]), y - 3, axis=0) + saved
    sums = gather_blocks(block.astype(BF16), z, x, c)

    mine = after(acts, tokens[1], tokens[2], tokens[3])
    own = key_grad.reshape(NY, TOK, HD)
    grads = [take(own, (y - j) % NY) for j in range(NY)]
    up = move_y(mine, 1)
    down = move_y(mine, -1)
    up, down = lax.optimization_barrier((up, down, summed))[:2]
    far_up = move_y(up[:64], 1)
    far_down = move_y(down[64:], -1)
    merged = feedback[0].astype(F32) + tdot(acts, grads[0])
    merged = merged + tdot(up, grads[1])
    merged = merged + tdot(down, grads[3])
    merged = merged + tdot(far_up, grads[2][:64])
    merged = merged + tdot(far_down, grads[2][64:])

    rebuilt, new_feedback, mean_factor = finish(
        sums.reshape(NC, NX * NZ, NY, 32, HD), factor_start, merged
    )

    by_head = jnp.roll(grad_rows[0].reshape(TOK, NY, HD).transpose(1, 0, 2), y, axis=0)
    other_by_head = move(by_head, dc=1)
    half_weight = after(take(key_weight.reshape(2, D // 2, HD), c), tokens[1], tokens[2], tokens[3])
    weights = lax.all_gather(half_weight, "tensor", axis=0)
    both = jnp.concatenate([by_head, other_by_head], axis=1)
    out = jnp.zeros((2 * TOK, D // 2), F32)
    for h in range(NY):
        out = out + lax.dot_general(
            both[h], weights[h], (((1,), (1,)), ((), ())), preferred_element_type=F32
        ).astype(BF16).astype(F32)
    out = out.astype(BF16)
    kept = out[:TOK]
    other = move(out[TOK:], dc=1)
    input_grad = jnp.concatenate(
        [jnp.where(c == 0, kept, other), jnp.where(c == 0, other, kept)], axis=1
    )
    return rebuilt, new_feedback[None], mean_factor, input_grad


def solution(mesh):
    return jax.shard_map(
        shards,
        mesh=mesh,
        in_specs=(
            P(("dp", "tensor"), None),
            P("dp", "tensor"),
            P(None, "tensor"),
            P("dp", None, "tensor"),
            P("tensor", None),
        ),
        out_specs=(
            P(None, "tensor"),
            P("dp", None, "tensor"),
            P("tensor", None),
            P(("dp", "tensor"), None),
        ),
        check_vma=False,
    )
```

```python
import jax
import jax.numpy as jnp
from jax import lax
from jax.experimental import pallas as pl
from jax.experimental.pallas import tpu as pltpu
from jax.sharding import PartitionSpec as P

BF16 = jnp.bfloat16
F32 = jnp.float32
HIGHEST = lax.Precision.HIGHEST
NZ, NX, NC, NY = 8, 4, 2, 4
D, HD, RANK, TOK, REPLICAS = 8192, 128, 64, 128, 64
HALF = D // NC
ROWS = HALF // (NX * NZ)
STEP = 1024
BLOCK = 2048


def move(value, dz=0, dx=0, dc=0):
    perm = []
    for z in range(NZ):
        for x in range(NX):
            for c in range(NC):
                target = (((z + dz) % NZ) * NX + (x + dx) % NX) * NC + (c + dc) % NC
                perm.append(((z * NX + x) * NC + c, target))
    return lax.ppermute(value, "dp", perm)


def move_y(value, dy):
    return lax.ppermute(value, "tensor", [(i, (i + dy) % NY) for i in range(NY)])


def take(blocks, index, axis=0):
    return lax.dynamic_index_in_dim(blocks, index, axis, keepdims=False)


def tdot(left, right):
    return lax.dot_general(left, right, (((0,), (0,)), ((), ())), preferred_element_type=F32)


def scratch_solve(sums, start_ref, factor_ref, high_ref, low_ref, rows_ref):
    gram_all = jnp.zeros((HD, HD), F32)
    for sums_ref in sums:
        for j in range(NX):
            rows = sums_ref[j].reshape(STEP, HD)
            gram_all = gram_all + tdot(rows, rows)
    start = start_ref[...]
    start_t = start.T
    projected = jnp.dot(start_t, gram_all, precision=HIGHEST, preferred_element_type=F32)
    gram = jnp.dot(projected, start, precision=HIGHEST, preferred_element_type=F32)
    table = jnp.concatenate([gram, gram, projected, start_t], axis=1)
    for k in range(RANK):
        base = k // 8 * 8
        table = table[-(RANK - base) :] if table.shape[0] > RANK - base else table
        local = k - base
        scale = 1.0 / jnp.sqrt(table[local : local + 1, k : k + 1])
        row = table[local : local + 1, :] * scale
        rows_ref[k : k + 1, :] = row[:, HD:]
        if k + 1 < RANK:
            column = table[:, k : k + 1] * scale
            below = lax.broadcasted_iota(jnp.int32, column.shape, 0) > local
            table = table - jnp.where(below, column, 0.0) * row
    right = rows_ref[:, :HD]
    left = rows_ref[:, HD:]
    kernel = lax.dot_general(
        left, right, (((0,), (0,)), ((), ())), precision=HIGHEST, preferred_element_type=F32
    ) * (1.0 / REPLICAS)
    factor_ref[...] = right.T * (1.0 / REPLICAS)
    high = kernel.astype(BF16)
    high_ref[...] = high
    low_ref[...] = (kernel - high.astype(F32)).astype(BF16)


def finish_kernel(place_ref, own_ref, other_ref, start_ref, kept_ref, away_ref, *refs):
    rebuilt_ref, feedback_ref, factor_ref, high_ref, low_ref, rows_ref = refs
    step = pl.program_id(0)

    @pl.when(step == 0)
    def _():
        scratch_solve((own_ref, other_ref), start_ref, factor_ref, high_ref, low_ref, rows_ref)

    per = HALF // BLOCK
    first = step % per * (NX // per)
    for side, (sums_ref, merged_ref) in enumerate(((own_ref, kept_ref), (other_ref, away_ref))):

        @pl.when(step // per == side)
        def _(sums_ref=sums_ref, merged_ref=merged_ref):
            blocks = [
                sums_ref[lax.rem(first + t + NX - place_ref[1], NX)] for t in range(NX // per)
            ]
            rows = jnp.concatenate([block.reshape(-1, HD) for block in blocks])
            rebuilt = jnp.dot(rows, high_ref[...], preferred_element_type=F32)
            rebuilt = rebuilt + jnp.dot(rows, low_ref[...], preferred_element_type=F32)
            rebuilt_ref[...] = rebuilt.astype(BF16)
            feedback_ref[...] = (merged_ref[...].astype(F32) - rebuilt).astype(BF16)


def finish(place, own, other, factor_start, kept, away):
    def whole(*shape):
        return pl.BlockSpec(shape, lambda i, p: (0,) * len(shape))

    per = HALF // BLOCK

    def placed(i, p):
        return (lax.rem(p[0] + i // per, NC) * per + i % per, 0)

    def side(first):
        return pl.BlockSpec((BLOCK, HD), lambda i, p: (jnp.clip(i - first, 0, per - 1), 0))

    block = pl.BlockSpec((BLOCK, HD), placed)
    sums = whole(NX, NZ, ROWS, HD)
    return pl.pallas_call(
        finish_kernel,
        grid_spec=pltpu.PrefetchScalarGridSpec(
            num_scalar_prefetch=1,
            grid=(D // BLOCK,),
            in_specs=[sums, sums, whole(HD, RANK), side(0), side(per)],
            out_specs=[block, block, whole(HD, RANK)],
            scratch_shapes=[
                pltpu.VMEM((HD, HD), BF16),
                pltpu.VMEM((HD, HD), BF16),
                pltpu.VMEM((RANK, 2 * HD), F32),
            ],
        ),
        out_shape=[
            jax.ShapeDtypeStruct((D, HD), BF16),
            jax.ShapeDtypeStruct((D, HD), BF16),
            jax.ShapeDtypeStruct((HD, RANK), F32),
        ],
        compiler_params=pltpu.CompilerParams(vmem_limit_bytes=24 * 2**20),
        cost_estimate=pl.CostEstimate(flops=10**9, bytes_accessed=12 * 2**20, transcendentals=0),
    )(place, own, other, factor_start, kept, away)


def reduce_x(acc, x):
    middle = acc.shape[1] // 2
    far = take(acc, (x + 2) % NX).astype(BF16)
    up = move(far[:middle], dx=1).astype(F32)
    down = move(far[middle:], dx=-1).astype(F32)
    right, left = take(acc, (x + 1) % NX), take(acc, (x + 3) % NX)
    right = jnp.concatenate([right[:middle] + up, right[middle:]]).astype(BF16)
    left = jnp.concatenate([left[:middle], left[middle:] + down]).astype(BF16)
    from_left = move(right, dx=1)
    from_right = move(left, dx=-1)
    return take(acc, x) + from_left.astype(F32) + from_right.astype(F32)


def reduce_z(acc, z):
    rel = {o: take(acc, (z + o) % NZ) for o in range(-4, 4)}
    up = move(jnp.stack([rel[2], rel[3], rel[-4]]).astype(BF16), dz=3).astype(F32)
    down = move(jnp.stack([rel[-2], rel[-3]]).astype(BF16), dz=-3).astype(F32)
    low = rel[-1] + up[0]
    own = rel[0] + up[1] + down[1]
    high = rel[1] + up[2] + down[0]
    from_below = move(high.astype(BF16), dz=1)
    from_above = move(low.astype(BF16), dz=-1)
    return own + from_below.astype(F32) + from_above.astype(F32)


def gather_z(block, z):
    below = move(block, dz=1)
    above = move(block, dz=-1)
    far_below = move(jnp.stack([below, block, above]), dz=3)
    far_above = move(jnp.stack([below, block]), dz=-3)
    ring = jnp.concatenate([far_below, jnp.stack([below, block, above]), far_above])
    return jnp.roll(ring, z - 4, axis=0)


def shards(acts, key_grad, key_weight, feedback, factor_start):
    barrier = lax.optimization_barrier
    dp = lax.axis_index("dp")
    y = lax.axis_index("tensor")
    z, x, c = dp // (NX * NC), (dp // NC) % NX, dp % NC
    quarters = key_grad.reshape(NY, TOK, HD)
    quarter = [take(quarters, (y + j) % NY) for j in range(NY)]
    middle = TOK // 2

    up, down = move_y(acts, 1), move_y(acts, -1)
    half = take(key_weight.reshape(NC, HALF, HD), c)
    near_up = jnp.concatenate([quarter[1], quarter[2][:middle], half])
    near_down = jnp.concatenate([half, quarter[2][middle:], quarter[3]])
    base = feedback[0].astype(F32) + tdot(acts, quarter[0])
    up, down, near_up, near_down, base = barrier((up, down, near_up, near_down, base))
    far_up = move_y(lax.dynamic_slice(up, (0, (1 - c) * HALF), (TOK, HALF)), 1)
    far_down = move_y(lax.dynamic_slice(down, (0, c * HALF), (TOK, HALF)), -1)
    base = base + tdot(up, quarter[3]) + tdot(down, quarter[1])
    sides = base.reshape(NC, HALF, HD)
    away = (take(sides, 1 - c) + tdot(far_up, quarter[2])).astype(BF16)
    received = move(away, dc=1)
    kept = take(sides, c) + tdot(far_down, quarter[2])
    acc = (kept + received.astype(F32)).reshape(NX, HALF // NX, HD)

    acc, near_up, near_down = barrier((acc, near_up, near_down))
    up, down = move_y(near_up, 1), move_y(near_down, -1)
    acc = reduce_x(acc, x)
    block = reduce_z(acc.reshape(NZ, ROWS, HD), z).astype(BF16)
    block, up, down = barrier((block, up, down))
    far_low = move_y(up[TOK : TOK + middle + HALF // 2], 1)
    far_high = move_y(down[HALF // 2 : HALF + middle], -1)
    column = gather_z(block, z)

    column, up, down, far_low, far_high = barrier((column, up, down, far_low, far_high))
    left, right = move(column, dx=1), move(column, dx=-1)
    heads = [quarter[0], up[:TOK], down[HALF + middle :]]
    heads.append(jnp.concatenate([far_low[:middle], far_high[HALF // 2 :]]))
    heads = jnp.stack(heads)
    both = jnp.concatenate([heads, move(heads, dc=1)], axis=1)
    weights = [half, up[TOK + middle :], down[:HALF]]
    weights.append(jnp.concatenate([far_low[middle:], far_high[: HALF // 2]]))
    out = jnp.zeros((NC * TOK, HALF), F32)
    for weight, head in zip(weights, both):
        out = out + lax.dot_general(
            head, weight, (((1,), (1,)), ((), ())), preferred_element_type=F32
        ).astype(BF16).astype(F32)
    out = out.astype(BF16)
    left, right, out = barrier((left, right, out))
    crossed = move(out[TOK:], dc=1)
    lower = NZ // 2
    far_left, far_right = move(left[:lower], dx=1), move(right[lower:], dx=-1)
    sums = jnp.stack([column, right, jnp.concatenate([far_left, far_right]), left])
    other = move(sums, dc=1)
    input_grad = jnp.where(
        c == 0,
        jnp.concatenate([out[:TOK], crossed], axis=1),
        jnp.concatenate([crossed, out[:TOK]], axis=1),
    )
    sums, other, input_grad = barrier((sums, other, input_grad))

    place = jnp.stack([c, x]).astype(jnp.int32)
    rebuilt, new_feedback, mean_factor = finish(place, sums, other, factor_start, kept, away)
    return rebuilt, new_feedback[None], mean_factor, input_grad


def solution(mesh):
    return jax.shard_map(
        shards,
        mesh=mesh,
        in_specs=(
            P(("dp", "tensor"), None),
            P("dp", "tensor"),
            P(None, "tensor"),
            P("dp", None, "tensor"),
            P("tensor", None),
        ),
        out_specs=(
            P(None, "tensor"),
            P("dp", None, "tensor"),
            P("tensor", None),
            P(("dp", "tensor"), None),
        ),
        check_vma=False,
    )
```

```python
import functools

import jax
import jax.numpy as jnp
from jax import lax
from jax.experimental import pallas as pl
from jax.experimental.pallas import tpu as pltpu
from jax.sharding import PartitionSpec as P

BF16 = jnp.bfloat16
F32 = jnp.float32
HIGHEST = lax.Precision.HIGHEST
NZ, NX, NC, NY = 8, 4, 2, 4
D, HD, RANK, TOK, REPLICAS = 8192, 128, 64, 128, 64
HALF = D // NC
ROWS = HALF // (NX * NZ)
BLOCK = 2048


def move(value, dz=0, dx=0, dc=0):
    perm = []
    for z in range(NZ):
        for x in range(NX):
            for c in range(NC):
                target = (((z + dz) % NZ) * NX + (x + dx) % NX) * NC + (c + dc) % NC
                perm.append(((z * NX + x) * NC + c, target))
    return lax.ppermute(value, "dp", perm)


def move_y(value, dy):
    return lax.ppermute(value, "tensor", [(i, (i + dy) % NY) for i in range(NY)])


def take(blocks, index, axis=0):
    return lax.dynamic_index_in_dim(blocks, index, axis, keepdims=False)


def tdot(left, right):
    return lax.dot_general(left, right, (((0,), (0,)), ((), ())), preferred_element_type=F32)


def scratch_solve(sums, start_ref, factor_ref, high_ref, low_ref, rows_ref):
    gram_all = jnp.zeros((HD, HD), F32)
    for sums_ref in sums:
        for j in range(NX):
            rows = sums_ref[j].reshape(-1, HD)
            gram_all = gram_all + tdot(rows, rows)
    start = start_ref[...]
    start_t = start.T
    projected = jnp.dot(start_t, gram_all, precision=HIGHEST, preferred_element_type=F32)
    gram = jnp.dot(projected, start, precision=HIGHEST, preferred_element_type=F32)
    table = jnp.concatenate([gram, gram, projected, start_t], axis=1)
    for k in range(RANK):
        base = k // 8 * 8
        table = table[-(RANK - base) :] if table.shape[0] > RANK - base else table
        local = k - base
        scale = 1.0 / jnp.sqrt(table[local : local + 1, k : k + 1])
        row = table[local : local + 1, :] * scale
        rows_ref[k : k + 1, :] = row[:, HD:]
        if k + 1 < RANK:
            column = table[:, k : k + 1] * scale
            below = lax.broadcasted_iota(jnp.int32, column.shape, 0) > local
            table = table - jnp.where(below, column, 0.0) * row
    right = rows_ref[:, :HD]
    left = rows_ref[:, HD:]
    kernel = lax.dot_general(
        left, right, (((0,), (0,)), ((), ())), precision=HIGHEST, preferred_element_type=F32
    ) * (1.0 / REPLICAS)
    factor_ref[...] = right.T * (1.0 / REPLICAS)
    high = kernel.astype(BF16)
    high_ref[...] = high
    low_ref[...] = (kernel - high.astype(F32)).astype(BF16)


def finish_kernel(
    place_ref, own_ref, other_ref, start_ref, grads_ref, kept_ref, away_ref, far_kept_ref, far_away_ref, *refs
):
    rebuilt_ref, feedback_ref, factor_ref, high_ref, low_ref, rows_ref = refs
    step = pl.program_id(0)

    @pl.when(step == 0)
    def _():
        scratch_solve((own_ref, other_ref), start_ref, factor_ref, high_ref, low_ref, rows_ref)

    per = HALF // BLOCK
    first = step % per * (NX // per)
    sides = ((own_ref, kept_ref, far_kept_ref), (other_ref, away_ref, far_away_ref))
    for side, (sums_ref, merged_ref, far_ref) in enumerate(sides):

        @pl.when(step // per == side)
        def _(sums_ref=sums_ref, merged_ref=merged_ref, far_ref=far_ref):
            blocks = [
                sums_ref[lax.rem(first + t + NX - place_ref[1], NX)] for t in range(NX // per)
            ]
            rows = jnp.concatenate([block.reshape(-1, HD) for block in blocks])
            rebuilt = jnp.dot(rows, high_ref[...], preferred_element_type=F32)
            rebuilt = rebuilt + jnp.dot(rows, low_ref[...], preferred_element_type=F32)
            rebuilt_ref[...] = rebuilt.astype(BF16)
            merged = merged_ref[...].astype(F32) + tdot(far_ref[...], grads_ref[...])
            feedback_ref[...] = (merged - rebuilt).astype(BF16)


def finish(place, own, other, factor_start, grads, kept, away, far_kept, far_away):
    def whole(*shape):
        return pl.BlockSpec(shape, lambda i, p: (0,) * len(shape))

    per = HALF // BLOCK

    def placed(i, p):
        return (lax.rem(p[0] + i // per, NC) * per + i % per, 0)

    def side(first):
        return pl.BlockSpec((BLOCK, HD), lambda i, p: (jnp.clip(i - first, 0, per - 1), 0))

    def far(first):
        return pl.BlockSpec((TOK, BLOCK), lambda i, p: (0, jnp.clip(i - first, 0, per - 1)))

    block = pl.BlockSpec((BLOCK, HD), placed)
    sums = whole(NX, NZ, ROWS, HD)
    return pl.pallas_call(
        finish_kernel,
        grid_spec=pltpu.PrefetchScalarGridSpec(
            num_scalar_prefetch=1,
            grid=(D // BLOCK,),
            in_specs=[
                sums,
                sums,
                whole(HD, RANK),
                whole(TOK, HD),
                side(0),
                side(per),
                far(0),
                far(per),
            ],
            out_specs=[block, block, whole(HD, RANK)],
            scratch_shapes=[
                pltpu.VMEM((HD, HD), BF16),
                pltpu.VMEM((HD, HD), BF16),
                pltpu.VMEM((RANK, 2 * HD), F32),
            ],
        ),
        out_shape=[
            jax.ShapeDtypeStruct((D, HD), BF16),
            jax.ShapeDtypeStruct((D, HD), BF16),
            jax.ShapeDtypeStruct((HD, RANK), F32),
        ],
        compiler_params=pltpu.CompilerParams(vmem_limit_bytes=24 * 2**20),
        cost_estimate=pl.CostEstimate(flops=10**9, bytes_accessed=12 * 2**20, transcendentals=0),
    )(place, own, other, factor_start, grads, kept, away, far_kept, far_away)


def reduce_x(block, x, *others):
    far = block((x + 2) % NX).astype(BF16)
    middle = far.shape[0] // 2
    up, down = move(far[:middle], dx=1), move(far[middle:], dx=-1)
    up, down, *others = lax.optimization_barrier((up, down, *others))
    up, down = up.astype(F32), down.astype(F32)
    right, left = block((x + 1) % NX), block((x + 3) % NX)
    right = jnp.concatenate([right[:middle] + up, right[middle:]]).astype(BF16)
    left = jnp.concatenate([left[:middle], left[middle:] + down]).astype(BF16)
    from_left = move(right, dx=1)
    from_right = move(left, dx=-1)
    return block(x) + from_left.astype(F32) + from_right.astype(F32), others


def reduce_z(acc, z, *others):
    rel = {o: take(acc, (z + o) % NZ) for o in range(-4, 4)}
    up = move(jnp.stack([rel[2], rel[3], rel[-4]]).astype(BF16), dz=3).astype(F32)
    down = move(jnp.stack([rel[-2], rel[-3]]).astype(BF16), dz=-3).astype(F32)
    low = rel[-1] + up[0]
    own = rel[0] + up[1] + down[1]
    high = rel[1] + up[2] + down[0]
    high, low, *others = lax.optimization_barrier((high.astype(BF16), low.astype(BF16), *others))
    from_below = move(high, dz=1)
    from_above = move(low, dz=-1)
    return own + from_below.astype(F32) + from_above.astype(F32), others


def gather_z(block, z, *others):
    below = move(block, dz=1)
    above = move(block, dz=-1)
    below, above, *others = lax.optimization_barrier((below, above, *others))
    far_below = move(jnp.stack([below, block, above]), dz=3)
    far_above = move(jnp.stack([below, block]), dz=-3)
    ring = jnp.concatenate([far_below, jnp.stack([below, block, above]), far_above])
    return jnp.roll(ring, z - 4, axis=0), others


def merge_kernel(count, core_ref, grads_ref, *refs):
    pieces, base, out_ref = refs[:count], refs[count:-1], refs[-1]
    total = base[0][...].astype(F32) if base else 0.0
    token = 0
    for piece in pieces:
        some = piece.shape[0]
        total = total + tdot(piece[...], grads_ref[token : token + some, :])
        token += some
    out_ref[...] = total.astype(out_ref.dtype)


def merge(core, grads, pieces, base, dtype):
    steps = HALF // BLOCK
    return pl.pallas_call(
        functools.partial(merge_kernel, len(pieces)),
        grid_spec=pltpu.PrefetchScalarGridSpec(
            num_scalar_prefetch=1,
            grid=(steps,),
            in_specs=[pl.BlockSpec(grads.shape, lambda i, p: (0, 0))]
            + [pl.BlockSpec((piece.shape[0], BLOCK), lambda i, p: (0, i)) for piece in pieces]
            + [pl.BlockSpec((BLOCK, HD), lambda i, p: (p[0] * steps + i, 0))] * len(base),
            out_specs=pl.BlockSpec((BLOCK, HD), lambda i, p: (i, 0)),
        ),
        out_shape=jax.ShapeDtypeStruct((HALF, HD), dtype),
        compiler_params=pltpu.CompilerParams(vmem_limit_bytes=16 * 2**20),
        cost_estimate=pl.CostEstimate(flops=5 * 10**8, bytes_accessed=4 * 2**20, transcendentals=0),
    )(core, grads, *pieces, *base)


def reduce_core_x(away, kept, x, *others):
    received = move(away, dc=1).reshape(NX, HALF // NX, HD)
    kept = kept.reshape(NX, HALF // NX, HD)
    return reduce_x(lambda i: take(kept, i).astype(F32) + take(received, i).astype(F32), x, *others)


def shards(acts, key_grad, key_weight, feedback, factor_start):
    barrier = lax.optimization_barrier
    dp = lax.axis_index("dp")
    y = lax.axis_index("tensor")
    z, x, c = dp // (NX * NC), (dp // NC) % NX, dp % NC
    here, there = c.reshape(1).astype(jnp.int32), (1 - c).reshape(1).astype(jnp.int32)
    quarters = key_grad.reshape(NY, TOK, HD)
    quarter = [take(quarters, (y + j) % NY) for j in range(NY)]

    across = move_y(quarter[2], 2)
    own_away = lax.dynamic_slice(acts, (0, (1 - c) * HALF), (TOK, HALF))
    own_kept = lax.dynamic_slice(acts, (0, c * HALF), (TOK, HALF))
    across, own_away, own_kept = barrier((across, own_away, own_kept))
    up_away, down_away = move_y(own_away, 1), move_y(own_away, -1)

    part, _ = reduce_core_x(
        merge(there, across, (own_away,), (), BF16), merge(here, across, (own_kept,), (), F32), x
    )
    up_away, down_away, own_kept = barrier((up_away, down_away, own_kept))
    up_kept, down_kept = move_y(own_kept, 1), move_y(own_kept, -1)
    part, up_away, down_away = barrier((part, up_away, down_away))
    part, _ = reduce_z(part.reshape(NZ, ROWS, HD), z)
    half = take(key_weight.reshape(NC, HALF, HD), c)
    near_up = jnp.concatenate([quarter[1], half])
    near_down = jnp.concatenate([half, quarter[3]])
    grads = jnp.concatenate([quarter[0], quarter[3], quarter[1]])
    saved = feedback[0]
    away = merge(there, grads, (own_away, up_away, down_away), (saved,), BF16)

    part, up_kept, down_kept, near_up, near_down, grads, away = barrier(
        (part, up_kept, down_kept, near_up, near_down, grads, away)
    )
    kept = merge(here, grads, (own_kept, up_kept, down_kept), (saved,), F32)
    acc, (part, near_up, near_down) = reduce_core_x(away, kept, x, move_y(part, 2), near_up, near_down)
    up, down = move_y(near_up, 1), move_y(near_down, -1)

    block, _ = reduce_z(acc.reshape(NZ, ROWS, HD), z)
    block, up, down = barrier((block + part, up, down))
    block = block.astype(BF16)
    far_low = move_y(up[TOK : TOK + HALF // 2], 1)
    far_high = move_y(down[HALF // 2 : HALF], -1)
    heads = jnp.stack([quarter[0], up[:TOK], down[HALF:], across])
    both = jnp.concatenate([heads, move(heads, dc=1)], axis=1)
    column, (up_away, down_kept) = gather_z(block, z, up_away, down_kept)
    far_away, far_kept = move_y(up_away, 1), move_y(down_kept, -1)
    column, far_low, far_high, both = barrier((column, far_low, far_high, both))

    left, right = move(column, dx=1), move(column, dx=-1)
    weights = [half, up[TOK:], down[:HALF], jnp.concatenate([far_low, far_high])]
    out = jnp.zeros((NC * TOK, HALF), F32)
    for weight, head in zip(weights, both):
        out = out + lax.dot_general(
            head, weight, (((1,), (1,)), ((), ())), preferred_element_type=F32
        ).astype(BF16).astype(F32)
    left, right, out = barrier((left, right, out.astype(BF16)))
    crossed = move(out[TOK:], dc=1)
    lower = NZ // 2
    far_left, far_right = move(left[:lower], dx=1), move(right[lower:], dx=-1)
    far_left, far_right, far_away, far_kept = barrier((far_left, far_right, far_away, far_kept))
    sums = jnp.stack([column, right, jnp.concatenate([far_left, far_right]), left])
    other = move(sums, dc=1)
    input_grad = jnp.where(
        c == 0,
        jnp.concatenate([out[:TOK], crossed], axis=1),
        jnp.concatenate([crossed, out[:TOK]], axis=1),
    )
    sums, other, input_grad = barrier((sums, other, input_grad))

    place = jnp.stack([c, x]).astype(jnp.int32)
    rebuilt, new_feedback, mean_factor = finish(
        place, sums, other, factor_start, quarter[2], kept, away, far_kept, far_away
    )
    return rebuilt, new_feedback[None], mean_factor, input_grad


def solution(mesh):
    return jax.shard_map(
        shards,
        mesh=mesh,
        in_specs=(
            P(("dp", "tensor"), None),
            P("dp", "tensor"),
            P(None, "tensor"),
            P("dp", None, "tensor"),
            P("tensor", None),
        ),
        out_specs=(
            P(None, "tensor"),
            P("dp", None, "tensor"),
            P("tensor", None),
            P(("dp", "tensor"), None),
        ),
        check_vma=False,
    )
```

```python
import functools

import jax
import jax.numpy as jnp
from jax import lax
from jax.experimental import pallas as pl
from jax.experimental.pallas import tpu as pltpu
from jax.sharding import PartitionSpec as P

BF16 = jnp.bfloat16
F32 = jnp.float32
HIGHEST = lax.Precision.HIGHEST
NZ, NX, NC, NY = 8, 4, 2, 4
D, HD, RANK, TOK, REPLICAS = 8192, 128, 64, 128, 64
HALF = D // NC
ROWS = HALF // (NX * NZ)
BLOCK = 2048


def move(value, dz=0, dx=0, dc=0):
    perm = []
    for z in range(NZ):
        for x in range(NX):
            for c in range(NC):
                target = (((z + dz) % NZ) * NX + (x + dx) % NX) * NC + (c + dc) % NC
                perm.append(((z * NX + x) * NC + c, target))
    return lax.ppermute(value, "dp", perm)


def move_y(value, dy):
    return lax.ppermute(value, "tensor", [(i, (i + dy) % NY) for i in range(NY)])


def take(blocks, index, axis=0):
    return lax.dynamic_index_in_dim(blocks, index, axis, keepdims=False)


def tdot(left, right):
    return lax.dot_general(left, right, (((0,), (0,)), ((), ())), preferred_element_type=F32)


def scratch_solve(sums, start_ref, factor_ref, high_ref, low_ref, rows_ref):
    gram_all = jnp.zeros((HD, HD), F32)
    for sums_ref in sums:
        for j in range(NX):
            rows = sums_ref[j].reshape(-1, HD)
            gram_all = gram_all + tdot(rows, rows)
    start = start_ref[...]
    start_t = start.T
    projected = jnp.dot(start_t, gram_all, precision=HIGHEST, preferred_element_type=F32)
    gram = jnp.dot(projected, start, precision=HIGHEST, preferred_element_type=F32)
    table = jnp.concatenate([gram, gram, projected, start_t], axis=1)
    for k in range(RANK):
        base = k // 8 * 8
        table = table[-(RANK - base) :] if table.shape[0] > RANK - base else table
        local = k - base
        pivot = table[local : local + 1, k : k + 1]
        row = table[local : local + 1, :]
        rows_ref[k : k + 1, :] = row[:, HD:] * (1.0 / jnp.sqrt(pivot))
        table = table - table[:, k : k + 1] * (row * (1.0 / pivot))
    right = rows_ref[:, :HD]
    left = rows_ref[:, HD:]
    kernel = lax.dot_general(
        left, right, (((0,), (0,)), ((), ())), precision=HIGHEST, preferred_element_type=F32
    ) * (1.0 / REPLICAS)
    factor_ref[...] = right.T * (1.0 / REPLICAS)
    high = kernel.astype(BF16)
    high_ref[...] = high
    low_ref[...] = (kernel - high.astype(F32)).astype(BF16)


def finish_kernel(
    place_ref, own_ref, other_ref, start_ref, grads_ref, kept_ref, away_ref, far_kept_ref, far_away_ref, *refs
):
    rebuilt_ref, feedback_ref, factor_ref, high_ref, low_ref, rows_ref = refs
    step = pl.program_id(0)

    @pl.when(step == 0)
    def _():
        scratch_solve((own_ref, other_ref), start_ref, factor_ref, high_ref, low_ref, rows_ref)

    per = HALF // BLOCK
    first = step % per * (NX // per)
    sides = ((own_ref, kept_ref, far_kept_ref), (other_ref, away_ref, far_away_ref))
    for side, (sums_ref, merged_ref, far_ref) in enumerate(sides):

        @pl.when(step // per == side)
        def _(sums_ref=sums_ref, merged_ref=merged_ref, far_ref=far_ref):
            blocks = [
                sums_ref[lax.rem(first + t + NX - place_ref[1], NX)] for t in range(NX // per)
            ]
            rows = jnp.concatenate([block.reshape(-1, HD) for block in blocks])
            rebuilt = jnp.dot(rows, high_ref[...], preferred_element_type=F32)
            rebuilt = rebuilt + jnp.dot(rows, low_ref[...], preferred_element_type=F32)
            rebuilt_ref[...] = rebuilt.astype(BF16)
            merged = merged_ref[...].astype(F32) + tdot(far_ref[...], grads_ref[...])
            feedback_ref[...] = (merged - rebuilt).astype(BF16)


def finish(place, own, other, factor_start, grads, kept, away, far_kept, far_away):
    def whole(*shape):
        return pl.BlockSpec(shape, lambda i, p: (0,) * len(shape))

    per = HALF // BLOCK

    def placed(i, p):
        return (lax.rem(p[0] + i // per, NC) * per + i % per, 0)

    def side(first):
        return pl.BlockSpec((BLOCK, HD), lambda i, p: (jnp.clip(i - first, 0, per - 1), 0))

    def far(first):
        return pl.BlockSpec((TOK, BLOCK), lambda i, p: (0, jnp.clip(i - first, 0, per - 1)))

    block = pl.BlockSpec((BLOCK, HD), placed)
    sums = whole(NX, NZ, ROWS, HD)
    return pl.pallas_call(
        finish_kernel,
        grid_spec=pltpu.PrefetchScalarGridSpec(
            num_scalar_prefetch=1,
            grid=(D // BLOCK,),
            in_specs=[
                sums,
                sums,
                whole(HD, RANK),
                whole(TOK, HD),
                side(0),
                side(per),
                far(0),
                far(per),
            ],
            out_specs=[block, block, whole(HD, RANK)],
            scratch_shapes=[
                pltpu.VMEM((HD, HD), BF16),
                pltpu.VMEM((HD, HD), BF16),
                pltpu.VMEM((RANK, 2 * HD), F32),
            ],
        ),
        out_shape=[
            jax.ShapeDtypeStruct((D, HD), BF16),
            jax.ShapeDtypeStruct((D, HD), BF16),
            jax.ShapeDtypeStruct((HD, RANK), F32),
        ],
        compiler_params=pltpu.CompilerParams(vmem_limit_bytes=24 * 2**20),
        cost_estimate=pl.CostEstimate(flops=10**9, bytes_accessed=12 * 2**20, transcendentals=0),
    )(place, own, other, factor_start, grads, kept, away, far_kept, far_away)


def reduce_x(block, x, *others):
    far = block((x + 2) % NX).astype(BF16)
    middle = far.shape[0] // 2
    up, down = move(far[:middle], dx=1), move(far[middle:], dx=-1)
    up, down, *others = lax.optimization_barrier((up, down, *others))
    up, down = up.astype(F32), down.astype(F32)
    right, left = block((x + 1) % NX), block((x + 3) % NX)
    right = jnp.concatenate([right[:middle] + up, right[middle:]]).astype(BF16)
    left = jnp.concatenate([left[:middle], left[middle:] + down]).astype(BF16)
    from_left = move(right, dx=1)
    from_right = move(left, dx=-1)
    return block(x) + from_left.astype(F32) + from_right.astype(F32), others


def reduce_z(acc, z, *others):
    rel = {o: take(acc, (z + o) % NZ) for o in range(-4, 4)}
    up = move(jnp.stack([rel[2], rel[3], rel[-4]]).astype(BF16), dz=3).astype(F32)
    down = move(jnp.stack([rel[-2], rel[-3]]).astype(BF16), dz=-3).astype(F32)
    low = rel[-1] + up[0]
    own = rel[0] + up[1] + down[1]
    high = rel[1] + up[2] + down[0]
    high, low, *others = lax.optimization_barrier((high.astype(BF16), low.astype(BF16), *others))
    from_below = move(high, dz=1)
    from_above = move(low, dz=-1)
    return own + from_below.astype(F32) + from_above.astype(F32), others


def gather_z(block, z, *others):
    below = move(block, dz=1)
    above = move(block, dz=-1)
    below, above, *others = lax.optimization_barrier((below, above, *others))
    far_below = move(jnp.stack([below, block, above]), dz=3)
    far_above = move(jnp.stack([below, block]), dz=-3)
    ring = jnp.concatenate([far_below, jnp.stack([below, block, above]), far_above])
    return jnp.roll(ring, z - 4, axis=0), others


def merge_kernel(count, core_ref, grads_ref, *refs):
    pieces, base, out_ref = refs[:count], refs[count:-1], refs[-1]
    total = base[0][...].astype(F32) if base else 0.0
    token = 0
    for piece in pieces:
        some = piece.shape[0]
        total = total + tdot(piece[...], grads_ref[token : token + some, :])
        token += some
    out_ref[...] = total.astype(out_ref.dtype)


def merge(core, grads, pieces, base, dtype):
    steps = HALF // BLOCK
    return pl.pallas_call(
        functools.partial(merge_kernel, len(pieces)),
        grid_spec=pltpu.PrefetchScalarGridSpec(
            num_scalar_prefetch=1,
            grid=(steps,),
            in_specs=[pl.BlockSpec(grads.shape, lambda i, p: (0, 0))]
            + [pl.BlockSpec((piece.shape[0], BLOCK), lambda i, p: (0, i)) for piece in pieces]
            + [pl.BlockSpec((BLOCK, HD), lambda i, p: (p[0] * steps + i, 0))] * len(base),
            out_specs=pl.BlockSpec((BLOCK, HD), lambda i, p: (i, 0)),
        ),
        out_shape=jax.ShapeDtypeStruct((HALF, HD), dtype),
        compiler_params=pltpu.CompilerParams(vmem_limit_bytes=16 * 2**20),
        cost_estimate=pl.CostEstimate(flops=5 * 10**8, bytes_accessed=4 * 2**20, transcendentals=0),
    )(core, grads, *pieces, *base)


def reduce_core_x(away, kept, x, *others):
    received = move(away, dc=1).reshape(NX, HALF // NX, HD)
    kept = kept.reshape(NX, HALF // NX, HD)
    return reduce_x(lambda i: take(kept, i).astype(F32) + take(received, i).astype(F32), x, *others)


def shards(acts, key_grad, key_weight, feedback, factor_start):
    barrier = lax.optimization_barrier
    dp = lax.axis_index("dp")
    y = lax.axis_index("tensor")
    z, x, c = dp // (NX * NC), (dp // NC) % NX, dp % NC
    here, there = c.reshape(1).astype(jnp.int32), (1 - c).reshape(1).astype(jnp.int32)
    quarters = key_grad.reshape(NY, TOK, HD)
    quarter = [take(quarters, (y + j) % NY) for j in range(NY)]

    across = move_y(quarter[2], 2)
    own_away = lax.dynamic_slice(acts, (0, (1 - c) * HALF), (TOK, HALF))
    own_kept = lax.dynamic_slice(acts, (0, c * HALF), (TOK, HALF))
    across, own_away, own_kept = barrier((across, own_away, own_kept))
    up_away, down_away = move_y(own_away, 1), move_y(own_away, -1)

    part, _ = reduce_core_x(
        merge(there, across, (own_away,), (), BF16), merge(here, across, (own_kept,), (), F32), x
    )
    up_away, down_away, own_kept = barrier((up_away, down_away, own_kept))
    up_kept, down_kept = move_y(own_kept, 1), move_y(own_kept, -1)
    part, up_away, down_away = barrier((part, up_away, down_away))
    part, _ = reduce_z(part.reshape(NZ, ROWS, HD), z)
    half = take(key_weight.reshape(NC, HALF, HD), c)
    near_up = jnp.concatenate([quarter[1], half])
    near_down = jnp.concatenate([half, quarter[3]])
    grads = jnp.concatenate([quarter[0], quarter[3], quarter[1]])
    saved = feedback[0]
    away = merge(there, grads, (own_away, up_away, down_away), (saved,), BF16)

    part, up_kept, down_kept, near_up, near_down, grads, away = barrier(
        (part, up_kept, down_kept, near_up, near_down, grads, away)
    )
    kept = merge(here, grads, (own_kept, up_kept, down_kept), (saved,), F32)
    acc, (part, near_up, near_down) = reduce_core_x(away, kept, x, move_y(part, 2), near_up, near_down)
    up, down = move_y(near_up, 1), move_y(near_down, -1)

    block, _ = reduce_z(acc.reshape(NZ, ROWS, HD), z)
    block, up, down = barrier((block + part, up, down))
    block = block.astype(BF16)
    far_low = move_y(up[TOK : TOK + HALF // 2], 1)
    far_high = move_y(down[HALF // 2 : HALF], -1)
    heads = jnp.stack([quarter[0], up[:TOK], down[HALF:], across])
    both = jnp.concatenate([heads, move(heads, dc=1)], axis=1)
    column, (up_away, down_kept) = gather_z(block, z, up_away, down_kept)
    far_away, far_kept = move_y(up_away, 1), move_y(down_kept, -1)
    column, far_low, far_high, both = barrier((column, far_low, far_high, both))

    left, right = move(column, dx=1), move(column, dx=-1)
    weights = [half, up[TOK:], down[:HALF], jnp.concatenate([far_low, far_high])]
    out = jnp.zeros((NC * TOK, HALF), F32)
    for weight, head in zip(weights, both):
        out = out + lax.dot_general(
            head, weight, (((1,), (1,)), ((), ())), preferred_element_type=F32
        ).astype(BF16).astype(F32)
    left, right, out = barrier((left, right, out.astype(BF16)))
    crossed = move(out[TOK:], dc=1)
    lower = NZ // 2
    far_left, far_right = move(left[:lower], dx=1), move(right[lower:], dx=-1)
    far_left, far_right, far_away, far_kept = barrier((far_left, far_right, far_away, far_kept))
    sums = jnp.stack([column, right, jnp.concatenate([far_left, far_right]), left])
    other = move(sums, dc=1)
    input_grad = jnp.where(
        c == 0,
        jnp.concatenate([out[:TOK], crossed], axis=1),
        jnp.concatenate([crossed, out[:TOK]], axis=1),
    )
    sums, other, input_grad = barrier((sums, other, input_grad))

    place = jnp.stack([c, x]).astype(jnp.int32)
    rebuilt, new_feedback, mean_factor = finish(
        place, sums, other, factor_start, quarter[2], kept, away, far_kept, far_away
    )
    return rebuilt, new_feedback[None], mean_factor, input_grad


def solution(mesh):
    return jax.shard_map(
        shards,
        mesh=mesh,
        in_specs=(
            P(("dp", "tensor"), None),
            P("dp", "tensor"),
            P(None, "tensor"),
            P("dp", None, "tensor"),
            P("tensor", None),
        ),
        out_specs=(
            P(None, "tensor"),
            P("dp", None, "tensor"),
            P("tensor", None),
            P(("dp", "tensor"), None),
        ),
        check_vma=False,
    )
```

```python
import functools

import jax
import jax.numpy as jnp
from jax import lax
from jax.experimental import pallas as pl
from jax.experimental.pallas import tpu as pltpu
from jax.sharding import PartitionSpec as P

BF16 = jnp.bfloat16
F32 = jnp.float32
HIGHEST = lax.Precision.HIGHEST
NZ, NX, NC, NY = 8, 4, 2, 4
D, HD, RANK, TOK, REPLICAS = 8192, 128, 64, 128, 64
HALF = D // NC
ROWS = HALF // (NX * NZ)
BLOCK = 2048


def move(value, dz=0, dx=0, dc=0):
    perm = []
    for z in range(NZ):
        for x in range(NX):
            for c in range(NC):
                target = (((z + dz) % NZ) * NX + (x + dx) % NX) * NC + (c + dc) % NC
                perm.append(((z * NX + x) * NC + c, target))
    return lax.ppermute(value, "dp", perm)


def move_y(value, dy):
    return lax.ppermute(value, "tensor", [(i, (i + dy) % NY) for i in range(NY)])


def take(blocks, index, axis=0):
    return lax.dynamic_index_in_dim(blocks, index, axis, keepdims=False)


def tdot(left, right):
    return lax.dot_general(left, right, (((0,), (0,)), ((), ())), preferred_element_type=F32)


def scratch_solve(sums, start_ref, factor_ref, high_ref, low_ref, rows_ref):
    gram_all = jnp.zeros((HD, HD), F32)
    for sums_ref in sums:
        for j in range(NX):
            rows = sums_ref[j].reshape(-1, HD)
            gram_all = gram_all + tdot(rows, rows)
    start = start_ref[...]
    start_t = start.T
    projected = jnp.dot(start_t, gram_all, precision=HIGHEST, preferred_element_type=F32)
    gram = jnp.dot(projected, start, precision=HIGHEST, preferred_element_type=F32)
    table = jnp.concatenate([gram, gram, projected, start_t], axis=1)
    for k in range(RANK):
        base = k // 8 * 8
        table = table[-(RANK - base) :] if table.shape[0] > RANK - base else table
        local = k - base
        pivot = table[local : local + 1, k : k + 1]
        row = table[local : local + 1, :]
        rows_ref[k : k + 1, :] = row[:, HD:] * (1.0 / jnp.sqrt(pivot))
        table = table - table[:, k : k + 1] * (row * (1.0 / pivot))
    right = rows_ref[:, :HD]
    left = rows_ref[:, HD:]
    kernel = lax.dot_general(
        left, right, (((0,), (0,)), ((), ())), precision=HIGHEST, preferred_element_type=F32
    ) * (1.0 / REPLICAS)
    factor_ref[...] = right.T * (1.0 / REPLICAS)
    high = kernel.astype(BF16)
    high_ref[...] = high
    low_ref[...] = (kernel - high.astype(F32)).astype(BF16)


def finish_kernel(
    place_ref, own_ref, other_ref, start_ref, grads_ref, kept_ref, away_ref, far_kept_ref, far_away_ref, *refs
):
    rebuilt_ref, feedback_ref, factor_ref, high_ref, low_ref, rows_ref = refs
    step = pl.program_id(0)

    @pl.when(step == 0)
    def _():
        scratch_solve((own_ref, other_ref), start_ref, factor_ref, high_ref, low_ref, rows_ref)

    per = HALF // BLOCK
    first = step % per * (NX // per)
    sides = ((own_ref, kept_ref, far_kept_ref), (other_ref, away_ref, far_away_ref))
    for side, (sums_ref, merged_ref, far_ref) in enumerate(sides):

        @pl.when(step // per == side)
        def _(sums_ref=sums_ref, merged_ref=merged_ref, far_ref=far_ref):
            blocks = [
                sums_ref[lax.rem(first + t + NX - place_ref[1], NX)] for t in range(NX // per)
            ]
            rows = jnp.concatenate([block.reshape(-1, HD) for block in blocks])
            rebuilt = jnp.dot(rows, high_ref[...], preferred_element_type=F32)
            rebuilt = rebuilt + jnp.dot(rows, low_ref[...], preferred_element_type=F32)
            rebuilt_ref[...] = rebuilt.astype(BF16)
            merged = merged_ref[...].astype(F32) + tdot(far_ref[...], grads_ref[...])
            feedback_ref[...] = (merged - rebuilt).astype(BF16)


def finish(place, own, other, factor_start, grads, kept, away, far_kept, far_away):
    def whole(*shape):
        return pl.BlockSpec(shape, lambda i, p: (0,) * len(shape))

    per = HALF // BLOCK

    def placed(i, p):
        return (lax.rem(p[0] + i // per, NC) * per + i % per, 0)

    def side(first):
        return pl.BlockSpec((BLOCK, HD), lambda i, p: (jnp.clip(i - first, 0, per - 1), 0))

    def far(first):
        return pl.BlockSpec((TOK, BLOCK), lambda i, p: (0, jnp.clip(i - first, 0, per - 1)))

    block = pl.BlockSpec((BLOCK, HD), placed)
    sums = whole(NX, NZ, ROWS, HD)
    return pl.pallas_call(
        finish_kernel,
        grid_spec=pltpu.PrefetchScalarGridSpec(
            num_scalar_prefetch=1,
            grid=(D // BLOCK,),
            in_specs=[
                sums,
                sums,
                whole(HD, RANK),
                whole(TOK, HD),
                side(0),
                side(per),
                far(0),
                far(per),
            ],
            out_specs=[block, block, whole(HD, RANK)],
            scratch_shapes=[
                pltpu.VMEM((HD, HD), BF16),
                pltpu.VMEM((HD, HD), BF16),
                pltpu.VMEM((RANK, 2 * HD), F32),
            ],
        ),
        out_shape=[
            jax.ShapeDtypeStruct((D, HD), BF16),
            jax.ShapeDtypeStruct((D, HD), BF16),
            jax.ShapeDtypeStruct((HD, RANK), F32),
        ],
        compiler_params=pltpu.CompilerParams(vmem_limit_bytes=24 * 2**20),
        cost_estimate=pl.CostEstimate(flops=10**9, bytes_accessed=12 * 2**20, transcendentals=0),
    )(place, own, other, factor_start, grads, kept, away, far_kept, far_away)


def reduce_x(block, x, *others):
    far = block((x + 2) % NX).astype(BF16)
    middle = far.shape[0] // 2
    up, down = move(far[:middle], dx=1), move(far[middle:], dx=-1)
    up, down, *others = lax.optimization_barrier((up, down, *others))
    up, down = up.astype(F32), down.astype(F32)
    right, left = block((x + 1) % NX), block((x + 3) % NX)
    right = jnp.concatenate([right[:middle] + up, right[middle:]]).astype(BF16)
    left = jnp.concatenate([left[:middle], left[middle:] + down]).astype(BF16)
    from_left = move(right, dx=1)
    from_right = move(left, dx=-1)
    return block(x) + from_left.astype(F32) + from_right.astype(F32), others


def reduce_z(acc, z, *others):
    rel = {o: take(acc, (z + o) % NZ) for o in range(-4, 4)}
    up = move(jnp.stack([rel[2], rel[3], rel[-4]]).astype(BF16), dz=3).astype(F32)
    down = move(jnp.stack([rel[-2], rel[-3]]).astype(BF16), dz=-3).astype(F32)
    low = rel[-1] + up[0]
    own = rel[0] + up[1] + down[1]
    high = rel[1] + up[2] + down[0]
    high, low, *others = lax.optimization_barrier((high.astype(BF16), low.astype(BF16), *others))
    from_below = move(high, dz=1)
    from_above = move(low, dz=-1)
    return own + from_below.astype(F32) + from_above.astype(F32), others


def gather_z(block, z, *others):
    below = move(block, dz=1)
    above = move(block, dz=-1)
    below, above, *others = lax.optimization_barrier((below, above, *others))
    far_below = move(jnp.stack([below, block, above]), dz=3)
    far_above = move(jnp.stack([below, block]), dz=-3)
    ring = jnp.concatenate([far_below, jnp.stack([below, block, above]), far_above])
    return jnp.roll(ring, z - 4, axis=0), others


def merge_kernel(count, core_ref, grads_ref, *refs):
    pieces, base, out_ref = refs[:count], refs[count:-1], refs[-1]
    total = base[0][...].astype(F32) if base else 0.0
    token = 0
    for piece in pieces:
        some = piece.shape[0]
        total = total + tdot(piece[...], grads_ref[token : token + some, :])
        token += some
    out_ref[...] = total.astype(out_ref.dtype)


def merge(core, grads, pieces, base, dtype):
    steps = HALF // BLOCK
    return pl.pallas_call(
        functools.partial(merge_kernel, len(pieces)),
        grid_spec=pltpu.PrefetchScalarGridSpec(
            num_scalar_prefetch=1,
            grid=(steps,),
            in_specs=[pl.BlockSpec(grads.shape, lambda i, p: (0, 0))]
            + [pl.BlockSpec((piece.shape[0], BLOCK), lambda i, p: (0, i)) for piece in pieces]
            + [pl.BlockSpec((BLOCK, HD), lambda i, p: (p[0] * steps + i, 0))] * len(base),
            out_specs=pl.BlockSpec((BLOCK, HD), lambda i, p: (i, 0)),
        ),
        out_shape=jax.ShapeDtypeStruct((HALF, HD), dtype),
        compiler_params=pltpu.CompilerParams(vmem_limit_bytes=16 * 2**20),
        cost_estimate=pl.CostEstimate(flops=5 * 10**8, bytes_accessed=4 * 2**20, transcendentals=0),
    )(core, grads, *pieces, *base)


def reduce_core_x(away, kept, x, *others):
    received = move(away, dc=1).reshape(NX, HALF // NX, HD)
    kept = kept.reshape(NX, HALF // NX, HD)
    return reduce_x(lambda i: take(kept, i).astype(F32) + take(received, i).astype(F32), x, *others)


def shards(acts, key_grad, key_weight, feedback, factor_start):
    barrier = lax.optimization_barrier
    dp = lax.axis_index("dp")
    y = lax.axis_index("tensor")
    z, x, c = dp // (NX * NC), (dp // NC) % NX, dp % NC
    here, there = c.reshape(1).astype(jnp.int32), (1 - c).reshape(1).astype(jnp.int32)
    quarters = key_grad.reshape(NY, TOK, HD)
    quarter = [take(quarters, (y + j) % NY) for j in range(NY)]

    across = move_y(quarter[2], 2)
    own_away = lax.dynamic_slice(acts, (0, (1 - c) * HALF), (TOK, HALF))
    own_kept = lax.dynamic_slice(acts, (0, c * HALF), (TOK, HALF))
    across, own_away, own_kept = barrier((across, own_away, own_kept))
    up_away, down_away = move_y(own_away, 1), move_y(own_away, -1)

    part, _ = reduce_core_x(
        merge(there, across, (own_away,), (), BF16), merge(here, across, (own_kept,), (), F32), x
    )
    up_away, down_away, own_kept = barrier((up_away, down_away, own_kept))
    up_kept, down_kept = move_y(own_kept, 1), move_y(own_kept, -1)
    part, up_away, down_away = barrier((part, up_away, down_away))
    part, _ = reduce_z(part.reshape(NZ, ROWS, HD), z)
    half = take(key_weight.reshape(NC, HALF, HD), c)
    near_up = jnp.concatenate([quarter[1], half])
    near_down = jnp.concatenate([half, quarter[3]])
    grads = jnp.concatenate([quarter[0], quarter[3], quarter[1]])
    saved = feedback[0]
    away = merge(there, grads, (own_away, up_away, down_away), (saved,), BF16)

    part, up_kept, down_kept, near_up, near_down, grads, away = barrier(
        (part, up_kept, down_kept, near_up, near_down, grads, away)
    )
    kept = merge(here, grads, (own_kept, up_kept, down_kept), (saved,), F32)
    acc, (part, near_up, near_down) = reduce_core_x(away, kept, x, move_y(part, 2), near_up, near_down)
    up, down = move_y(near_up, 1), move_y(near_down, -1)

    block, _ = reduce_z(acc.reshape(NZ, ROWS, HD), z)
    block, up, down = barrier((block + part, up, down))
    block = block.astype(BF16)
    far_low = move_y(up[TOK : TOK + HALF // 2], 1)
    far_high = move_y(down[HALF // 2 : HALF], -1)
    heads = jnp.stack([quarter[0], up[:TOK], down[HALF:], across])
    both = jnp.concatenate([heads, move(heads, dc=1)], axis=1)
    column, (up_away, down_kept) = gather_z(block, z, up_away, down_kept)
    far_away, far_kept = move_y(up_away, 1), move_y(down_kept, -1)
    column, far_low, far_high, both = barrier((column, far_low, far_high, both))

    left, right = move(column, dx=1), move(column, dx=-1)
    weights = [half, up[TOK:], down[:HALF], jnp.concatenate([far_low, far_high])]
    out = jnp.zeros((NC * TOK, HALF), F32)
    for weight, head in zip(weights, both):
        out = out + lax.dot_general(
            head, weight, (((1,), (1,)), ((), ())), preferred_element_type=F32
        ).astype(BF16).astype(F32)
    left, right, out = barrier((left, right, out.astype(BF16)))
    crossed = move(out[TOK:], dc=1)
    lower = NZ // 2
    far_left, far_right = move(left[:lower], dx=1), move(right[lower:], dx=-1)
    sums = jnp.stack([column, right, jnp.concatenate([far_left, far_right]), left])
    other = move(sums, dc=1)
    input_grad = jnp.where(
        c == 0,
        jnp.concatenate([out[:TOK], crossed], axis=1),
        jnp.concatenate([crossed, out[:TOK]], axis=1),
    )
    sums, other, input_grad = barrier((sums, other, input_grad))

    place = jnp.stack([c, x]).astype(jnp.int32)
    rebuilt, new_feedback, mean_factor = finish(
        place, sums, other, factor_start, quarter[2], kept, away, far_kept, far_away
    )
    return rebuilt, new_feedback[None], mean_factor, input_grad


def solution(mesh):
    return jax.shard_map(
        shards,
        mesh=mesh,
        in_specs=(
            P(("dp", "tensor"), None),
            P("dp", "tensor"),
            P(None, "tensor"),
            P("dp", None, "tensor"),
            P("tensor", None),
        ),
        out_specs=(
            P(None, "tensor"),
            P("dp", None, "tensor"),
            P("tensor", None),
            P(("dp", "tensor"), None),
        ),
        check_vma=False,
    )
```
